128 devices in a mesh: leaf: 32 (over y, z, core), sep: 4 (over x).
Axes of the slice: x: 4, y: 4, z: 4, core: 2. Of those that a mesh axis runs over, the one named last changes fastest.
Arguments:
- leaf_rhs: float32 [56, 524288], P(None, ('leaf', 'sep')), may hold values from -6 to 6
- leaf_inverse: float32 [1024, 512, 512], P(('leaf', 'sep')), may hold values from -2 to 2, as said below
- leaf_update: float32 [1024, 256, 512], P(('leaf', 'sep')), may hold values from -0.0546875 to 0.0546875
- leaf_rows: int32 [1024, 256], P(('leaf', 'sep')), may hold values from 0 to 65535, as said below
- sep_rhs: float32 [56, 65536], P(None, ('leaf', 'sep')), may hold values from -6 to 6
- sep_inverse: float32 [2048, 65536], P(None, ('leaf', 'sep')), may hold values from -2 to 2, as said below
- sep_update: float32 [65536, 2048], P(('leaf', 'sep')), may hold values from -0.0625 to 0.0625
Outputs:
- leaf_solution: float32 [56, 524288], P(None, ('leaf', 'sep'))
- sep_solution: float32 [56, 65536], P(None, ('leaf', 'sep'))
The draws below stay inside these ranges and needn't reach their ends.
Inputs may be any that keep to these rules, and one draw needn't show every extreme that they name: Each 512 x 512 block of leaf_inverse is lower triangular with a positive diagonal. Each 2048 x 2048 block of sep_inverse is lower triangular with a positive diagonal. leaf_rows[j, r] = a * 2048 + i with 0 <= i < 2048, where a is the home of an ancestor separator of the leaf supernode's subtree: the leaf index of block j is floor(j / 32) = l, and a is the level-k home of l, floor(l / 2^k) * 2^k + 2^(k-1) for some k in 1..5, or 0. Entries may repeat.
All inputs are finite; a program needn't handle non-finite values.
Results may differ from the reference program's by a relative error of at most 0.0003.
Values sent between devices are 32-bit elements; how exact they have to be, the bound alone decides.
No kernel may reach another device: no remote copies, remote signals or barrier semaphores. Data moves between devices by JAX's collectives and lax.ppermute only.
A program may use at most 192 MiB of HBM per device.

```python
import math
import jax
import jax.numpy as jnp
from jax import lax

K = 56
NB = 512
RL = 256
NS = 2048
LEVELS = 5
BLOCKS = 1024
N_LEAF = 32


def triangle(offdiag, diagonal):
    size_now = offdiag.shape[-1]
    row_ids = lax.broadcasted_iota(jnp.int32, (size_now, size_now), 0)
    col_ids = lax.broadcasted_iota(jnp.int32, (size_now, size_now), 1)
    lower_part = jnp.where(row_ids > col_ids, offdiag, 0.0)
    on_diagonal = jnp.where(row_ids == col_ids, 1.0, 0.0) * diagonal[..., None]
    return lower_part + on_diagonal


def draw_leaf_inverse(key, part):
    key = jax.random.fold_in(key, 3)
    key_off, key_diag = jax.random.split(key)
    offdiag = jnp.clip(jax.random.normal(key_off, (BLOCKS, NB, NB), jnp.float32), -6.0, 6.0) * (0.5 / math.sqrt(NB))
    diagonal = jnp.exp(jax.random.uniform(key_diag, (BLOCKS, NB), jnp.float32, math.log(0.5), math.log(2.0)))
    return triangle(offdiag, diagonal)


def draw_sep_inverse(key, part):
    key = jax.random.fold_in(key, 5)
    key_off, key_diag = jax.random.split(key)
    members = 2 ** LEVELS
    offdiag = jnp.clip(jax.random.normal(key_off, (members, NS, NS), jnp.float32), -6.0, 6.0) * (0.5 / math.sqrt(NS))
    diagonal = jnp.exp(jax.random.uniform(key_diag, (members, NS), jnp.float32, math.log(0.5), math.log(2.0)))
    blocks_out = triangle(offdiag, diagonal)
    return jnp.transpose(blocks_out, (1, 0, 2)).reshape(NS, members * NS)


def draw_leaf_rows(key, part):
    key = jax.random.fold_in(key, 7)
    key_level, key_row = jax.random.split(key)
    members = 2 ** LEVELS
    per_leaf = BLOCKS // members
    drawn = jax.random.randint(key_level, (BLOCKS, RL), 1, 2 ** (LEVELS + 1), jnp.int32)
    magnitude = jnp.zeros((BLOCKS, RL), jnp.int32)
    for power in range(1, LEVELS + 1):
        magnitude = magnitude + (drawn >= 2 ** power).astype(jnp.int32)
    target_level = LEVELS + 1 - magnitude
    leaf_index = (lax.broadcasted_iota(jnp.int32, (BLOCKS, RL), 0) // per_leaf).astype(jnp.int32)
    span = jnp.left_shift(jnp.ones((BLOCKS, RL), jnp.int32), target_level)
    homes = jnp.where(target_level == LEVELS + 1, 0, leaf_index // span * span + span // 2)
    within = jax.random.randint(key_row, (BLOCKS, RL), 0, NS, jnp.int32)
    return (homes * NS + within).astype(jnp.int32)


def levels(rng, dims, shards, low, top_value):
    factor_of = 1.0
    for position, blocks in shards:
        heights = jax.random.uniform(jax.random.fold_in(jax.random.fold_in(rng, 6), position), (blocks,), jnp.float32, low / len(shards), top_value / len(shards))
        factor_of = factor_of * jnp.repeat(jnp.exp(heights), dims[position] // blocks).reshape((-1,) + (1,) * (len(dims) - 1 - position))
    return factor_of


def centred(stream_key, extent, scale, most, pieces=(), kind=jnp.bfloat16):
    array = scale * jax.random.normal(stream_key, extent, jnp.float32)
    if pieces:
        array = array * levels(stream_key, extent, pieces, -0.22, 0.18)
    return jnp.clip(array, -most, most).astype(kind)


def setup_inputs(seed: int = 0) -> dict:
    keys = jax.random.split(jax.random.key(seed), 8)
    leaf_rhs = centred(keys[0], (K, BLOCKS * NB), 1.0, 6.0, ((1, 128),), jnp.float32)
    leaf_inverse = draw_leaf_inverse(jax.random.fold_in(keys[7], 71), 0)
    leaf_update = centred(keys[2], (BLOCKS, RL, NB), (25 * NB) ** -0.5, 0.0546875, ((0, 128),), jnp.float32)
    leaf_rows = draw_leaf_rows(jax.random.fold_in(keys[7], 71), 0)
    sep_rhs = centred(keys[4], (K, N_LEAF * NS), 1.0, 6.0, ((1, 128),), jnp.float32)
    sep_inverse = draw_sep_inverse(jax.random.fold_in(keys[7], 71), 0)
    sep_update = centred(keys[6], (N_LEAF * NS, NS), (4 * NS) ** -0.5, 0.0625, ((0, 128),), jnp.float32)
    return {"leaf_rhs": leaf_rhs, "leaf_inverse": leaf_inverse, "leaf_update": leaf_update, "leaf_rows": leaf_rows, "sep_rhs": sep_rhs, "sep_inverse": sep_inverse, "sep_update": sep_update}


def level_of(home_index, depth):
    if home_index == 0:
        return depth + 1
    result = 1
    while home_index % 2 == 0:
        home_index = home_index // 2
        result = result + 1
    return result


def parent_of(home_index, section, depth):
    reach = 2 ** (section - 1)
    if section == depth:
        return 0
    if (home_index // (2 * reach)) % 2 == 0:
        return home_index + reach
    return home_index - reach


def reference(leaf_rhs, leaf_inverse, leaf_update, leaf_rows, sep_rhs, sep_inverse, sep_update):
    exact = lax.Precision.HIGHEST
    members = 2 ** LEVELS
    blocks_in = leaf_rhs.reshape(K, BLOCKS, NB)
    leaf_forward = jnp.einsum('kjm,jim->kji', blocks_in, leaf_inverse, precision=exact, preferred_element_type=jnp.float32)
    leaf_terms = jnp.einsum('kji,jri->kjr', leaf_forward, leaf_update, precision=exact, preferred_element_type=jnp.float32)
    flat_rows = leaf_rows.reshape(-1)
    spread = jnp.zeros((K, members * NS), jnp.float32).at[:, flat_rows].add(leaf_terms.reshape(K, -1))
    pending = sep_rhs - spread
    order = sorted(range(members), key=lambda item: level_of(item, LEVELS))
    forward = {}
    for home_index in order:
        section = level_of(home_index, LEVELS)
        inverse = sep_inverse[:, home_index * NS:(home_index + 1) * NS]
        solved = jnp.dot(pending[:, home_index * NS:(home_index + 1) * NS], inverse.T, precision=exact, preferred_element_type=jnp.float32)
        forward[home_index] = solved
        if section <= LEVELS:
            parent = parent_of(home_index, section, LEVELS)
            update = sep_update[home_index * NS:(home_index + 1) * NS, :]
            moved = jnp.dot(solved, update.T, precision=exact, preferred_element_type=jnp.float32)
            pending = pending.at[:, parent * NS:(parent + 1) * NS].add(-moved)
    solution = {}
    for home_index in reversed(order):
        section = level_of(home_index, LEVELS)
        inverse = sep_inverse[:, home_index * NS:(home_index + 1) * NS]
        through = forward[home_index]
        if section <= LEVELS:
            parent = parent_of(home_index, section, LEVELS)
            update = sep_update[home_index * NS:(home_index + 1) * NS, :]
            through = through - jnp.dot(solution[parent], update, precision=exact, preferred_element_type=jnp.float32)
        solution[home_index] = jnp.dot(through, inverse, precision=exact, preferred_element_type=jnp.float32)
    sep_solution = jnp.concatenate([solution[item] for item in range(members)], axis=1)
    targets = sep_solution[:, flat_rows].reshape(K, BLOCKS, RL)
    leaf_through = leaf_forward - jnp.einsum('kjr,jri->kji', targets, leaf_update, precision=exact, preferred_element_type=jnp.float32)
    leaf_solution = jnp.einsum('kji,jim->kjm', leaf_through, leaf_inverse, precision=exact, preferred_element_type=jnp.float32)
    return leaf_solution.reshape(K, BLOCKS * NB), sep_solution
```

```python
import functools

import jax
import jax.numpy as jnp
from jax import lax
from jax.experimental import pallas as pl
from jax.experimental.pallas import tpu as pltpu
from jax.sharding import PartitionSpec as P

JOINT = ("leaf", "sep")
PAD = 64
F32 = jnp.float32
BF16 = jnp.bfloat16


def halves(value):
    high = value.astype(BF16)
    low = (value - high.astype(F32)).astype(BF16)
    return high, low


def stacked(value):
    rows, width = value.shape
    padded = jnp.concatenate([value, jnp.zeros((PAD - rows, width), F32)], axis=0)
    high, low = halves(padded)
    return jnp.concatenate([high, low], axis=0)


def product(left, weights, contract):
    high, low = halves(weights)
    dims = (((1,), (contract,)), ((), ()))
    total = lax.dot_general(left, high, dims, preferred_element_type=F32)
    return total + lax.dot_general(left, low, dims, preferred_element_type=F32)


def folded(total, rows):
    return total[:rows] + total[PAD : PAD + rows]


def spread_kernel(blocks, rows_ref, rhs_ref, inv_ref, upd_ref, fwd_ref, *rest):
    outs, (acc_a, acc_b, terms) = rest[:4], rest[4:]
    step = pl.program_id(0)
    scenarios = rhs_ref.shape[0]
    count = upd_ref.shape[1]

    @pl.when(step == 0)
    def _():
        acc_a[...] = jnp.zeros_like(acc_a)
        acc_b[...] = jnp.zeros_like(acc_b)

    forward = folded(product(stacked(rhs_ref[...]), inv_ref[0], 1), scenarios)
    fwd_ref[...] = forward
    left = stacked(forward)
    high, low = halves(upd_ref[0])
    dims = (((1,), (1,)), ((), ()))
    total = lax.dot_general(high, left, dims, preferred_element_type=F32)
    total = total + lax.dot_general(low, left, dims, preferred_element_type=F32)
    terms[...] = total + pltpu.roll(total, PAD, 1)

    def add_rows(index, carry):
        first = index * 16
        for offset in range(16):
            acc = acc_a if offset % 2 == 0 else acc_b
            row = rows_ref[step, first + offset]
            acc[pl.ds(row, 1), :] += terms[pl.ds(first + offset, 1), :]
        return carry

    lax.fori_loop(0, count // 16, add_rows, 0)

    @pl.when(step == blocks - 1)
    def _():
        width = outs[0].shape[-1]
        place = 0
        for out in outs:
            flat = [(g, b) for g in range(out.shape[0]) for b in range(out.shape[1])]
            for g, b in flat:
                piece = acc_a[pl.ds(place, width), :] + acc_b[pl.ds(place, width), :]
                out[g, b] = piece.T[:scenarios]
                place += width


def leaf_spread(rows, leaf_rhs, leaf_inverse, leaf_update, width):
    scenarios = leaf_rhs.shape[0]
    blocks, size, _ = leaf_inverse.shape
    count = leaf_update.shape[1]
    groups = [1, 2, 1, 2]
    total = sum(groups) * 4 * width
    shapes = [jax.ShapeDtypeStruct((g, 4, scenarios, width), F32) for g in groups]
    return pl.pallas_call(
        functools.partial(spread_kernel, blocks),
        grid_spec=pltpu.PrefetchScalarGridSpec(
            num_scalar_prefetch=1,
            grid=(blocks,),
            in_specs=[
                pl.BlockSpec((scenarios, size), lambda j, r: (0, j)),
                pl.BlockSpec((1, size, size), lambda j, r: (j, 0, 0)),
                pl.BlockSpec((1, count, size), lambda j, r: (j, 0, 0)),
            ],
            out_specs=[pl.BlockSpec((scenarios, size), lambda j, r: (0, j))]
            + [pl.BlockSpec(x.shape, lambda j, r: (0, 0, 0, 0)) for x in shapes],
            scratch_shapes=[
                pltpu.VMEM((total, 128), F32),
                pltpu.VMEM((total, 128), F32),
                pltpu.VMEM((count, 128), F32),
            ],
        ),
        out_shape=[jax.ShapeDtypeStruct(leaf_rhs.shape, F32)] + shapes,
        compiler_params=pltpu.CompilerParams(vmem_limit_bytes=50 * 2**20),
    )(rows, leaf_rhs, leaf_inverse, leaf_update)


def finish_kernel(rows_ref, fwd_ref, inv_ref, upd_ref, m1, p1, m2, p2, out_ref, table, found):
    step = pl.program_id(0)
    scenarios = fwd_ref.shape[0]
    count = upd_ref.shape[1]

    @pl.when(step == 0)
    def _():
        width = m1.shape[-1]
        place = 0
        for source in (m1, p1, m2, p2):
            for g in range(source.shape[0]):
                for b in range(source.shape[1]):
                    piece = jnp.concatenate(
                        [source[g, b], jnp.zeros((128 - scenarios, width), F32)], axis=0
                    )
                    table[pl.ds(place, width), :] = piece.T
                    place += width

    def take_rows(index, carry):
        first = index * 16
        for offset in range(16):
            row = rows_ref[step, first + offset]
            found[pl.ds(first + offset, 1), :] = table[pl.ds(row, 1), :]
        return carry

    lax.fori_loop(0, count // 16, take_rows, 0)
    targets = found[...].T[:scenarios]
    through = fwd_ref[...] - folded(product(stacked(targets), upd_ref[0], 0), scenarios)
    out_ref[...] = folded(product(stacked(through), inv_ref[0], 0), scenarios)


def leaf_finish(rows, forward, leaf_inverse, leaf_update, sources):
    scenarios = forward.shape[0]
    blocks, size, _ = leaf_inverse.shape
    count = leaf_update.shape[1]
    total = sum(x.shape[0] * x.shape[1] * x.shape[3] for x in sources)
    return pl.pallas_call(
        finish_kernel,
        grid_spec=pltpu.PrefetchScalarGridSpec(
            num_scalar_prefetch=1,
            grid=(blocks,),
            in_specs=[
                pl.BlockSpec((scenarios, size), lambda j, r: (0, j)),
                pl.BlockSpec((1, size, size), lambda j, r: (j, 0, 0)),
                pl.BlockSpec((1, count, size), lambda j, r: (j, 0, 0)),
            ]
            + [pl.BlockSpec(x.shape, lambda j, r: (0, 0, 0, 0)) for x in sources],
            out_specs=pl.BlockSpec((scenarios, size), lambda j, r: (0, j)),
            scratch_shapes=[pltpu.VMEM((total, 128), F32), pltpu.VMEM((count, 128), F32)],
        ),
        out_shape=jax.ShapeDtypeStruct(forward.shape, F32),
        compiler_params=pltpu.CompilerParams(vmem_limit_bytes=50 * 2**20),
    )(rows, forward, leaf_inverse, leaf_update, *sources)


def parts_kernel(contract, place_ref, x_ref, w_ref, out_ref):
    rows = x_ref.shape[0]
    out_ref[0] = folded(product(stacked(x_ref[...]), w_ref[...], contract), rows)


def sum_kernel(contract, steps, place_ref, x_ref, w_ref, out_ref):
    step = pl.program_id(0)
    rows = out_ref.shape[0]
    value = folded(product(stacked(x_ref[0]), w_ref[...], contract), rows)

    @pl.when(step == 0)
    def _():
        out_ref[...] = value

    @pl.when(step > 0)
    def _():
        out_ref[...] += value


def to_parts(place, x, weights, long_dim, contract):
    rows, width = x.shape
    index = (lambda j, p: ((p[0] + j) % 4, 0)) if long_dim == 0 else (lambda j, p: (0, (p[0] + j) % 4))
    return pl.pallas_call(
        functools.partial(parts_kernel, contract),
        grid_spec=pltpu.PrefetchScalarGridSpec(
            num_scalar_prefetch=1,
            grid=(4,),
            in_specs=[
                pl.BlockSpec((rows, width), lambda j, p: (0, 0)),
                pl.BlockSpec((width, width), index),
            ],
            out_specs=pl.BlockSpec((1, rows, width), lambda j, p: (j, 0, 0)),
        ),
        out_shape=jax.ShapeDtypeStruct((4, rows, width), F32),
    )(place, x, weights)


def from_parts(place, x, weights, long_dim, contract):
    _, rows, width = x.shape
    index = (
        (lambda j, p: ((p[0] + 4 - j) % 4, 0))
        if long_dim == 0
        else (lambda j, p: (0, (p[0] + 4 - j) % 4))
    )
    return pl.pallas_call(
        functools.partial(sum_kernel, contract, 4),
        grid_spec=pltpu.PrefetchScalarGridSpec(
            num_scalar_prefetch=1,
            grid=(4,),
            in_specs=[
                pl.BlockSpec((1, rows, width), lambda j, p: (j, 0, 0)),
                pl.BlockSpec((width, width), index),
            ],
            out_specs=pl.BlockSpec((rows, width), lambda j, p: (0, 0)),
        ),
        out_shape=jax.ShapeDtypeStruct((rows, width), F32),
    )(place, x, weights)


def swapped(value, mask, chosen=None):
    count = lax.axis_size("leaf")
    pairs = [(a, a ^ mask) for a in range(count) if chosen is None or chosen(a)]
    return lax.ppermute(value, "leaf", pairs)


def shifted(value, steps):
    count = lax.axis_size("sep")
    return lax.ppermute(value, "sep", [(a, (a + steps) % count) for a in range(count)])


def sep_reduced(parts):
    return (
        parts[0] + shifted(parts[1], 1) + shifted(parts[2], 2) + shifted(parts[3], 3)
    )


def sep_gathered(share):
    return jnp.stack([share, shifted(share, 1), shifted(share, 2), shifted(share, 3)])


def static_level(a):
    level = 1
    for bit in range(5):
        level += a % 2 ** (bit + 1) == 0
    return level


def level_of(index_now):
    total = jnp.ones_like(index_now)
    for bit in range(5):
        total = total + (index_now % 2 ** (bit + 1) == 0).astype(jnp.int32)
    return total


def on_device(leaf_rhs, leaf_inverse, leaf_update, leaf_rows, sep_rhs, sep_inverse, sep_update):
    scenarios, quarter = sep_rhs.shape
    width = sep_update.shape[1]
    home = lax.axis_index("leaf")
    member = lax.axis_index("sep")
    core = home % 2
    level = level_of(home)
    place = member.reshape(1).astype(jnp.int32)

    row_home, within = leaf_rows // width, leaf_rows % width
    part, rest = within // quarter, within % quarter
    at = level_of(row_home)
    slot_even = jnp.where(at == 1, 3, jnp.where(at >= 5, at - 1, at - 2))
    slot_odd = jnp.where(at == 1, 0, jnp.where(at >= 5, at - 4, at + 1))
    add_at = (
        jnp.where(core == 0, slot_even, slot_odd) * width + (part - member) % 4 * quarter + rest
    )
    slot_even = jnp.where(
        at == 1, 5, jnp.where(at == 4, 4, jnp.where(at >= 5, at - 3, at - 2))
    )
    slot_odd = jnp.where(at == 1, 4, jnp.where(at == 4, 5, jnp.where(at >= 5, at - 5, at)))
    take_at = (
        jnp.where(core == 0, slot_even, slot_odd) * width + (member - part) % 4 * quarter + rest
    )

    leaf_forward, keep_first, keep_rest, send_first, send_rest = leaf_spread(
        add_at, leaf_rhs, leaf_inverse, leaf_update, quarter
    )
    first = keep_first[0] + swapped(send_first[0], 1)
    others = keep_rest + swapped(send_rest, 1)
    first = sep_reduced(first)
    others = sep_reduced([others[:, j] for j in range(4)])

    pending = sep_rhs - jnp.where(level == 1, first, 0.0)

    arrived = swapped(jnp.concatenate([first[None], others]), 2)
    level_two = first + arrived[0]
    others = others + arrived[1:]
    others = others + swapped(others, 4)
    level_three = others[0]
    others = others + swapped(others, 8)
    level_four = others[1]
    others = others + swapped(others, 16)
    top_two = swapped(jnp.where(home == 17, others[0], others[1]), 1)
    pending = pending - jnp.where(
        level == 1,
        0.0,
        jnp.where(
            level == 2,
            level_two,
            jnp.where(level == 3, level_three, jnp.where(level == 4, level_four, top_two)),
        ),
    )
    pending_one = sep_rhs - first

    own_forward = jnp.zeros_like(sep_rhs)
    for section in range(1, 7):
        current = pending_one if section == 1 else pending
        share = sep_reduced(to_parts(place, current, sep_inverse, 0, 1))
        own_forward = jnp.where(level == section, share, own_forward)
        if section < 6:
            moved = from_parts(place, sep_gathered(share), sep_update, 1, 1)
            reach = 2 ** (section - 1)
            incoming = swapped(moved, reach)
            if section < 5:
                incoming = incoming + swapped(moved, 3 * reach)
            else:
                incoming = swapped(moved, 16)
            pending = pending - jnp.where(level == section + 1, incoming, 0.0)

    own_solution = jnp.zeros_like(sep_rhs)
    above = None
    for section in range(6, 0, -1):
        if section == 6:
            through = own_forward
        else:
            reach = 2 ** (section - 1)
            sender = lambda a: static_level(a) == section + 1
            if section < 5:
                left_side = home // (2 * reach) % 2 == 0

                def from_parent(value, chosen=None):
                    return jnp.where(
                        left_side, swapped(value, 3 * reach, chosen), swapped(value, reach, chosen)
                    )
            else:

                def from_parent(value, chosen=None):
                    return swapped(value, 16, chosen)

            parent = from_parent(own_solution)
            if above is None:
                above = parent[None]
            else:
                above = jnp.concatenate([parent[None], from_parent(above, sender)])
            through = own_forward - sep_reduced(to_parts(place, parent, sep_update, 1, 0))
        result = from_parts(place, sep_gathered(through), sep_inverse, 0, 0)
        own_solution = jnp.where(level == section, result, own_solution)

    above = jnp.where(core == 0, swapped(above, 1), above)
    early = jnp.where(core == 0, above[0:2], above[3:5])
    early = jnp.swapaxes(sep_gathered(early), 0, 1)
    late = sep_gathered(jnp.where(core == 0, above[2], own_solution))[None]
    leaf_solution = leaf_finish(
        take_at,
        leaf_forward,
        leaf_inverse,
        leaf_update,
        [early, swapped(early, 1), late, swapped(late, 1)],
    )
    return leaf_solution, own_solution


def solution(mesh):
    return jax.shard_map(
        on_device,
        mesh=mesh,
        in_specs=(
            P(None, JOINT),
            P(JOINT, None, None),
            P(JOINT, None, None),
            P(JOINT, None),
            P(None, JOINT),
            P(None, JOINT),
            P(JOINT, None),
        ),
        out_specs=(P(None, JOINT), P(None, JOINT)),
        check_vma=False,
    )
```

```python
import functools

import jax
import jax.numpy as jnp
from jax import lax
from jax.experimental import pallas as pl
from jax.experimental.pallas import tpu as pltpu
from jax.sharding import PartitionSpec as P

JOINT = ("leaf", "sep")
PAD = 64
F32 = jnp.float32
BF16 = jnp.bfloat16


def halves(value):
    high = value.astype(BF16)
    low = (value - high.astype(F32)).astype(BF16)
    return high, low


def stacked(value):
    rows, width = value.shape
    padded = jnp.concatenate([value, jnp.zeros((PAD - rows, width), F32)], axis=0)
    high, low = halves(padded)
    return jnp.concatenate([high, low], axis=0)


def product(left, weights, contract):
    high, low = halves(weights)
    dims = (((1,), (contract,)), ((), ()))
    total = lax.dot_general(left, high, dims, preferred_element_type=F32)
    return total + lax.dot_general(left, low, dims, preferred_element_type=F32)


def folded(total, rows):
    return total[:rows] + total[PAD : PAD + rows]


def spread_kernel(blocks, rows_ref, rhs_ref, inv_ref, upd_ref, fwd_ref, *rest):
    outs, (acc_a, acc_b, terms_a, terms_b) = rest[:2], rest[2:]
    step = pl.program_id(0)
    scenarios = rhs_ref.shape[0]
    count = upd_ref.shape[1]

    @pl.when(step == 0)
    def _():
        acc_a[...] = jnp.zeros_like(acc_a)
        acc_b[...] = jnp.zeros_like(acc_b)
        terms_b[...] = jnp.zeros_like(terms_b)

    def block(old, new):
        before = jnp.maximum(step - 1, 0)
        for index in range(count):
            acc = acc_a if index % 2 == 0 else acc_b
            row = rows_ref[before, index]
            acc[pl.ds(row, 1), :] += old[pl.ds(index, 1), :]
        forward = folded(product(stacked(rhs_ref[...]), inv_ref[0], 1), scenarios)
        fwd_ref[...] = forward
        left = stacked(forward)
        high, low = halves(upd_ref[0])
        dims = (((1,), (1,)), ((), ()))
        total = lax.dot_general(high, left, dims, preferred_element_type=F32)
        total = total + lax.dot_general(low, left, dims, preferred_element_type=F32)
        new[...] = total + pltpu.roll(total, PAD, 1)

    @pl.when(step % 2 == 0)
    def _():
        block(terms_b, terms_a)

    @pl.when(step % 2 == 1)
    def _():
        block(terms_a, terms_b)

    @pl.when(step == blocks)
    def _():
        width = outs[0].shape[-1]
        place = 0
        for out in outs:
            flat = [(g, b) for g in range(out.shape[0]) for b in range(out.shape[1])]
            for g, b in flat:
                piece = acc_a[pl.ds(place, width), :] + acc_b[pl.ds(place, width), :]
                out[g, b] = piece.T[:scenarios]
                place += width


def leaf_spread(rows, leaf_rhs, leaf_inverse, leaf_update, width):
    scenarios = leaf_rhs.shape[0]
    blocks, size, _ = leaf_inverse.shape
    count = leaf_update.shape[1]
    groups = [2, 4]
    total = sum(groups) * 4 * width
    shapes = [jax.ShapeDtypeStruct((4, g, scenarios, width), F32) for g in groups]
    return pl.pallas_call(
        functools.partial(spread_kernel, blocks),
        grid_spec=pltpu.PrefetchScalarGridSpec(
            num_scalar_prefetch=1,
            grid=(blocks + 1,),
            in_specs=[
                pl.BlockSpec((scenarios, size), lambda j, r: (0, jnp.minimum(j, blocks - 1))),
                pl.BlockSpec((1, size, size), lambda j, r: (jnp.minimum(j, blocks - 1), 0, 0)),
                pl.BlockSpec((1, count, size), lambda j, r: (jnp.minimum(j, blocks - 1), 0, 0)),
            ],
            out_specs=[pl.BlockSpec((scenarios, size), lambda j, r: (0, jnp.minimum(j, blocks - 1)))]
            + [pl.BlockSpec(x.shape, lambda j, r: (0, 0, 0, 0)) for x in shapes],
            scratch_shapes=[
                pltpu.VMEM((total, 128), F32),
                pltpu.VMEM((total, 128), F32),
                pltpu.VMEM((count, 128), F32),
                pltpu.VMEM((count, 128), F32),
            ],
        ),
        out_shape=[jax.ShapeDtypeStruct(leaf_rhs.shape, F32)] + shapes,
        compiler_params=pltpu.CompilerParams(vmem_limit_bytes=50 * 2**20),
    )(rows, leaf_rhs, leaf_inverse, leaf_update)


def finish_kernel(
    blocks, rows_ref, fwd_ref, inv_ref, upd_ref, mine, other, out_ref, table, found_a, found_b
):
    step = pl.program_id(0)
    scenarios = fwd_ref.shape[0]
    count = upd_ref.shape[1]

    @pl.when(step == 0)
    def _():
        width = mine.shape[-1]
        place = 0
        for source in (mine, other):
            for g in range(source.shape[0]):
                for b in range(source.shape[1]):
                    piece = jnp.concatenate(
                        [source[g, b], jnp.zeros((128 - scenarios, width), F32)], axis=0
                    )
                    table[pl.ds(place, width), :] = piece.T
                    place += width
        found_b[...] = jnp.zeros_like(found_b)

    def block(old, new):
        after = jnp.minimum(step, blocks - 1)
        for index in range(count):
            row = rows_ref[after, index]
            new[pl.ds(index, 1), :] = table[pl.ds(row, 1), :]
        targets = old[...].T[:scenarios]
        through = fwd_ref[...] - folded(product(stacked(targets), upd_ref[0], 0), scenarios)
        out_ref[...] = folded(product(stacked(through), inv_ref[0], 0), scenarios)

    @pl.when(step % 2 == 0)
    def _():
        block(found_b, found_a)

    @pl.when(step % 2 == 1)
    def _():
        block(found_a, found_b)


def leaf_finish(rows, forward, leaf_inverse, leaf_update, sources):
    scenarios = forward.shape[0]
    blocks, size, _ = leaf_inverse.shape
    count = leaf_update.shape[1]
    total = sum(x.shape[0] * x.shape[1] * x.shape[3] for x in sources)
    return pl.pallas_call(
        functools.partial(finish_kernel, blocks),
        grid_spec=pltpu.PrefetchScalarGridSpec(
            num_scalar_prefetch=1,
            grid=(blocks + 1,),
            in_specs=[
                pl.BlockSpec((scenarios, size), lambda j, r: (0, jnp.maximum(j - 1, 0))),
                pl.BlockSpec((1, size, size), lambda j, r: (jnp.maximum(j - 1, 0), 0, 0)),
                pl.BlockSpec((1, count, size), lambda j, r: (jnp.maximum(j - 1, 0), 0, 0)),
            ]
            + [pl.BlockSpec(x.shape, lambda j, r: (0, 0, 0, 0)) for x in sources],
            out_specs=pl.BlockSpec((scenarios, size), lambda j, r: (0, jnp.maximum(j - 1, 0))),
            scratch_shapes=[pltpu.VMEM((total, 128), F32)] + [pltpu.VMEM((count, 128), F32)] * 2,
        ),
        out_shape=jax.ShapeDtypeStruct(forward.shape, F32),
        compiler_params=pltpu.CompilerParams(vmem_limit_bytes=50 * 2**20),
    )(rows, forward, leaf_inverse, leaf_update, *sources)


def chain_kernel(mode, contract, long_dim, count, place_ref, *refs):
    x_refs, w_ref = refs[:count], refs[count]
    outs = refs[count + 1 : count + (5 if mode == "parts" else 2)]
    held, sems = refs[-2:]
    rows, width = x_refs[0].shape
    copies = []
    for j in range(4):
        if long_dim is None:
            source = w_ref.at[j]
        else:
            block = (place_ref[0] + (j if mode == "parts" else 4 - j)) % 4
            span = pl.ds(pl.multiple_of(block * width, width), width)
            source = w_ref.at[span, :] if long_dim == 0 else w_ref.at[:, span]
        copies.append(pltpu.make_async_copy(source, held.at[j], sems.at[j]))
        copies[-1].start()
    dims = (((1,), (contract,)), ((), ()))
    left = [stacked(x[...]) for x in x_refs]
    total = None
    for j in range(4):
        copies[j].wait()
        if long_dim is None:
            high, low = held[j, 0], held[j, 1]
        else:
            high, low = halves(held[j])
        mine = left[j % count]
        value = lax.dot_general(mine, high, dims, preferred_element_type=F32)
        value = value + lax.dot_general(mine, low, dims, preferred_element_type=F32)
        if mode == "parts":
            outs[j][...] = folded(value, rows)
        else:
            total = value if total is None else total + value
    if mode == "sum":
        outs[0][...] = folded(total, rows)


def chain_product(place, xs, weights, long_dim, contract, mode):
    rows, width = xs[0].shape
    number = 4 if mode == "parts" else 1
    held = (
        pltpu.VMEM((4, 2, width, width), BF16)
        if long_dim is None
        else pltpu.VMEM((4, width, width), F32)
    )
    whole = pl.BlockSpec(memory_space=pltpu.VMEM)
    result = pl.pallas_call(
        functools.partial(chain_kernel, mode, contract, long_dim, len(xs)),
        in_specs=[pl.BlockSpec(memory_space=pltpu.SMEM)]
        + [whole] * len(xs)
        + [pl.BlockSpec(memory_space=pltpu.HBM)],
        out_specs=[whole] * number,
        out_shape=[jax.ShapeDtypeStruct((rows, width), F32)] * number,
        scratch_shapes=[held, pltpu.SemaphoreType.DMA((4,))],
        compiler_params=pltpu.CompilerParams(vmem_limit_bytes=16 * 2**20),
        cost_estimate=pl.CostEstimate(
            flops=16 * rows * width * width, bytes_accessed=4 * 2**20, transcendentals=0
        ),
    )(place, *xs, weights)
    return result if mode == "parts" else result[0]


def squared_kernel(place_ref, *refs):
    x_refs, own_ref, after, far_upper, far_lower, before, out_ref, held, kept, sems = refs
    rows, width = out_ref.shape
    slots = held.shape[0]
    jobs = []
    for j, source in ((0, (own_ref,)), (1, (after,)), (3, (before,)), (2, (far_upper, far_lower))):
        each = 4 // len(source)
        for i in range(4):
            jobs.append((j, i, source[i // each].at[pl.ds(i % each * width, width), :]))
    copies = []
    for number, (j, i, block) in enumerate(jobs):
        target = kept.at[i] if number < 4 else held.at[number % slots]
        sem = sems.at[number % slots] if number >= 4 else sems.at[slots + number]
        copies.append(pltpu.make_async_copy(block, target, sem))
    for number in range(4 + slots):
        copies[number].start()
    left = [stacked(x[...]) for x in x_refs]
    totals = [None] * 4
    for number, (j, i, _) in enumerate(jobs):
        copies[number].wait()
        weights = kept[i] if number < 4 else held[number % slots]
        value = product(left[j], weights, 1)
        totals[i] = value if totals[i] is None else totals[i] + value
        if number >= 4 and number + slots < len(jobs):
            copies[number + slots].start()
    result = None
    for i in range(4):
        value = product(stacked(folded(totals[i], rows)), kept[i], 0)
        result = value if result is None else result + value
    out_ref[...] = folded(result, rows)


def squared_product(place, xs, own, others):
    rows, width = xs[0].shape
    slots = 4
    whole = pl.BlockSpec(memory_space=pltpu.VMEM)
    far = pl.BlockSpec(memory_space=pltpu.HBM)

    def body(place_ref, *refs):
        squared_kernel(place_ref, list(refs[:4]), *refs[4:])

    return pl.pallas_call(
        body,
        in_specs=[pl.BlockSpec(memory_space=pltpu.SMEM)] + [whole] * 4 + [far] * 5,
        out_specs=whole,
        out_shape=jax.ShapeDtypeStruct((rows, width), F32),
        scratch_shapes=[
            pltpu.VMEM((slots, width, width), F32),
            pltpu.VMEM((4, width, width), F32),
            pltpu.SemaphoreType.DMA((slots + 4,)),
        ],
        compiler_params=pltpu.CompilerParams(vmem_limit_bytes=24 * 2**20),
        cost_estimate=pl.CostEstimate(
            flops=80 * rows * width * width, bytes_accessed=16 * 2**20, transcendentals=0
        ),
    )(place, *xs, own, *others)


def half_copies(flag, after, before):
    rows, width = after.shape
    half = rows // 2

    def body(flag_ref, after_ref, before_ref, upper_ref, lower_ref, held, sems):
        @pl.when(flag_ref[0] == 1)
        def _():
            sources = after_ref.at[pl.ds(0, half), :], before_ref.at[pl.ds(half, half), :]
            inward = [pltpu.make_async_copy(sources[k], held.at[k], sems.at[k]) for k in (0, 1)]
            outward = [
                pltpu.make_async_copy(held.at[k], (upper_ref, lower_ref)[k], sems.at[2 + k])
                for k in (0, 1)
            ]
            for k in (0, 1):
                inward[k].start()
            for k in (0, 1):
                inward[k].wait()
                outward[k].start()
            for k in (0, 1):
                outward[k].wait()

    far = pl.BlockSpec(memory_space=pltpu.HBM)
    return pl.pallas_call(
        body,
        in_specs=[pl.BlockSpec(memory_space=pltpu.SMEM), far, far],
        out_specs=[far, far],
        out_shape=[jax.ShapeDtypeStruct((half, width), F32)] * 2,
        scratch_shapes=[pltpu.VMEM((2, half, width), F32), pltpu.SemaphoreType.DMA((4,))],
        compiler_params=pltpu.CompilerParams(vmem_limit_bytes=16 * 2**20),
    )(flag, after, before)


def merged(flag, a, pieces, place, held):
    width = pieces[0].shape[1]
    extra = [] if held is None else [held]

    def body(flag_ref, a_ref, *refs):
        sources = refs[: len(pieces)]
        out_ref, left_held, right_held, result, sems = refs[len(pieces) + len(extra) :]

        @pl.when(flag_ref[0] == 1)
        def _():
            copies = []
            for i in range(4):
                each = 4 // len(sources)
                block = sources[i // each].at[pl.ds(i % each * width, width), :]
                copies.append(
                    (
                        pltpu.make_async_copy(
                            a_ref.at[:, pl.ds(i * width, width)], left_held.at[i], sems.at[2 * i]
                        ),
                        pltpu.make_async_copy(block, right_held.at[i], sems.at[2 * i + 1]),
                    )
                )
                for copy in copies[-1]:
                    copy.start()
            total = None
            dims = (((1,), (0,)), ((), ()))
            for i in range(4):
                for copy in copies[i]:
                    copy.wait()
                left, right = halves(left_held[i]), halves(right_held[i])
                for x, y in ((0, 0), (0, 1), (1, 0)):
                    term = lax.dot_general(left[x], right[y], dims, preferred_element_type=F32)
                    total = term if total is None else total + term
            high, low = halves(total)
            result[0] = high
            result[1] = low
            back = pltpu.make_async_copy(result, out_ref.at[place], sems.at[8])
            back.start()
            back.wait()

    far = pl.BlockSpec(memory_space=pltpu.HBM)
    return pl.pallas_call(
        body,
        in_specs=[pl.BlockSpec(memory_space=pltpu.SMEM)] + [far] * (1 + len(pieces) + len(extra)),
        out_specs=far,
        out_shape=jax.ShapeDtypeStruct((4, 2, width, width), BF16),
        scratch_shapes=[
            pltpu.VMEM((4, width, width), F32),
            pltpu.VMEM((4, width, width), F32),
            pltpu.VMEM((2, width, width), BF16),
            pltpu.SemaphoreType.DMA((9,)),
        ],
        input_output_aliases={} if held is None else {2 + len(pieces): 0},
        compiler_params=pltpu.CompilerParams(vmem_limit_bytes=24 * 2**20),
        cost_estimate=pl.CostEstimate(
            flops=24 * width**3, bytes_accessed=10 * 2**20, transcendentals=0
        ),
    )(flag, a, *pieces, *extra)


def joint_sent(value, pairs, core):
    count = lax.axis_size("leaf")
    full = [(a * 4 + x, a * 4 + y) for a in range(core, count, 2) for x, y in pairs]
    return lax.ppermute(value, JOINT, full)


def bulk_sent(value, steps, core):
    return joint_sent(value, [(x, (x + steps) % 4) for x in range(4)], core)


def swapped(value, mask, chosen=None):
    count = lax.axis_size("leaf")
    pairs = [(a, a ^ mask) for a in range(count) if chosen is None or chosen(a)]
    return lax.ppermute(value, "leaf", pairs)


def shifted(value, steps):
    count = lax.axis_size("sep")
    return lax.ppermute(value, "sep", [(a, (a + steps) % count) for a in range(count)])


def odd_shifted(value, steps):
    return joint_sent(value, [(x, (x + steps) % 4) for x in range(4)], 1)


def even_shifted(value, steps):
    return joint_sent(value, [(x, (x + steps) % 4) for x in range(4)], 0)


def sep_reduced(parts, sign=1, move=shifted):
    total = parts[0]
    for steps in (1, 2, 3):
        total = total + move(parts[steps], sign * steps % 4)
    return total


def sep_gathered(share, move=shifted):
    return [share, move(share, 1), move(share, 2), move(share, 3)]


def static_level(a):
    level = 1
    for bit in range(5):
        level += a % 2 ** (bit + 1) == 0
    return level


def level_of(index_now):
    total = jnp.ones_like(index_now)
    for bit in range(5):
        total = total + (index_now % 2 ** (bit + 1) == 0).astype(jnp.int32)
    return total


def on_device(leaf_rhs, leaf_inverse, leaf_update, leaf_rows, sep_rhs, sep_inverse, sep_update):
    scenarios, quarter = sep_rhs.shape
    width = sep_update.shape[1]
    home = lax.axis_index("leaf")
    member = lax.axis_index("sep")
    core = home % 2
    level = level_of(home)
    place = member.reshape(1).astype(jnp.int32)

    row_home, within = leaf_rows // width, leaf_rows % width
    part, rest = within // quarter, within % quarter
    at = level_of(row_home)
    turn = (part - member) % 4
    slot = jnp.where(at <= 2, turn * 2 + at - 1, turn * 4 + at + 5)
    add_at = slot * quarter + rest
    is_even = (at >= 2) & (at <= 4)
    slot = jnp.where(is_even, at - 2, jnp.where(at == 1, 0, at - 4))
    theirs = (is_even != (core == 0)).astype(jnp.int32)
    take_at = (theirs * 12 + (member - part) % 4 * 3 + slot) * quarter + rest

    leaf_forward, low, high = leaf_spread(
        add_at, leaf_rhs, leaf_inverse, leaf_update, quarter
    )
    low = low + swapped(low, 1)
    high = high + swapped(high, 1)
    even = lambda a: a % 2 == 0
    high = high + swapped(high, 2, even)

    flag = (core == 0).astype(jnp.int32).reshape(1)
    half = width // 2
    after = bulk_sent(sep_inverse, 1, 0)
    before = bulk_sent(sep_inverse, 3, 0)
    update = merged(flag, sep_update, [sep_inverse], 0, None)
    low, update, after, before = lax.optimization_barrier((low, update, after, before))

    low = sep_reduced([low[j] for j in range(4)], move=odd_shifted)
    one = chain_product(place, [sep_rhs - low[0]], sep_inverse, 0, 1, "parts")
    halves_out = half_copies(flag, after, before)
    halves_out, update = lax.optimization_barrier((halves_out, update))
    far_upper = bulk_sent(halves_out[0], 1, 0)
    far_lower = bulk_sent(halves_out[1], 3, 0)
    update = merged(flag, sep_update, [after], 1, update)
    high = high + swapped(high, 4, even)
    high, update = lax.optimization_barrier((high, update))
    high = [high[0]] + [even_shifted(high[j], j) for j in (1, 2, 3)]
    update = merged(flag, sep_update, [before], 3, update)
    update = merged(flag, sep_update, [far_upper, far_lower], 2, update)
    high, update = lax.optimization_barrier((high, update))
    high = high[0] + high[1] + high[2] + high[3]

    forward_one = sep_reduced(one, move=odd_shifted)
    moved = chain_product(place, sep_gathered(forward_one, odd_shifted), sep_update, 1, 1, "sum")
    moved = moved + low[1]
    moved, update, high = lax.optimization_barrier((moved, update, high))
    moved = swapped(moved + swapped(moved, 2), 1)

    def to_parent(moved, section):
        reach = 2 ** (section - 1)
        if section == 5:
            return swapped(moved, 16)
        return swapped(moved, reach) + swapped(moved, 3 * reach)

    def from_parent(value, section, chosen=None):
        reach = 2 ** (section - 1)
        if section == 5:
            return swapped(value, 16, chosen)
        left_side = home // (2 * reach) % 2 == 0
        return jnp.where(
            left_side, swapped(value, 3 * reach, chosen), swapped(value, reach, chosen)
        )

    pending = sep_rhs - jnp.where(level == 2, moved, 0.0)
    for section in range(2, 6):
        moved = chain_product(place, sep_gathered(pending), update, None, 1, "sum")
        moved, high = lax.optimization_barrier((moved, high))
        if section == 2:
            spread = {3: high[0]}
            high = high[1:] + swapped(high[1:], 8, even)
        elif section == 3:
            spread[4] = high[0]
            high = high[1:] + swapped(high[1:], 16, even)
            spread[5], spread[6] = high[0], high[1]
        arriving = to_parent(moved, section) + spread[section + 1]
        pending = pending - jnp.where(level == section + 1, arriving, 0.0)
    squared = squared_product(
        place, sep_gathered(pending), sep_inverse, [after, far_upper, far_lower, before]
    )

    own_solution = squared
    above = None
    for section in range(5, 0, -1):
        parent = from_parent(own_solution, section)
        if section == 1:
            above = from_parent(above, section, chosen=lambda a: static_level(a) == 2)
            above = jnp.concatenate([parent[None], above])
            above = jnp.where(core == 0, swapped(above, 1), above)
        elif above is None:
            above = parent[None]
        else:
            chosen = lambda a: static_level(a) == section + 1
            above = jnp.concatenate([parent[None], from_parent(above, section, chosen)])
        if section > 1:
            result = squared - sep_reduced(
                chain_product(place, [parent], update, None, 0, "parts"), -1
            )
        else:
            through = forward_one - sep_reduced(
                chain_product(place, [parent], sep_update, 1, 0, "parts")
            )
            result = chain_product(place, sep_gathered(through), sep_inverse, 0, 0, "sum")
        own_solution = jnp.where(level == section, result, own_solution)

    own_three = jnp.concatenate([own_solution[None], above[3:5]])
    mine = jnp.stack(sep_gathered(jnp.where(core == 0, above[0:3], own_three)))
    leaf_solution = leaf_finish(
        take_at,
        leaf_forward,
        leaf_inverse,
        leaf_update,
        [mine, swapped(mine, 1)],
    )
    return leaf_solution, own_solution


def solution(mesh):
    return jax.shard_map(
        on_device,
        mesh=mesh,
        in_specs=(
            P(None, JOINT),
            P(JOINT, None, None),
            P(JOINT, None, None),
            P(JOINT, None),
            P(None, JOINT),
            P(None, JOINT),
            P(JOINT, None),
        ),
        out_specs=(P(None, JOINT), P(None, JOINT)),
        check_vma=False,
    )
```

```python
import functools

import jax
import jax.numpy as jnp
from jax import lax
from jax.experimental import pallas as pl
from jax.experimental.pallas import tpu as pltpu
from jax.sharding import PartitionSpec as P

JOINT = ("leaf", "sep")
PAD = 64
F32 = jnp.float32
BF16 = jnp.bfloat16


def halves(value):
    high = value.astype(BF16)
    low = (value - high.astype(F32)).astype(BF16)
    return high, low


def stacked(value):
    rows, width = value.shape
    padded = jnp.concatenate([value, jnp.zeros((PAD - rows, width), F32)], axis=0)
    high, low = halves(padded)
    return jnp.concatenate([high, low], axis=0)


def product(left, weights, contract):
    high, low = halves(weights)
    dims = (((1,), (contract,)), ((), ()))
    total = lax.dot_general(left, high, dims, preferred_element_type=F32)
    return total + lax.dot_general(left, low, dims, preferred_element_type=F32)


def folded(total, rows):
    return total[:rows] + total[PAD : PAD + rows]


def spread_kernel(blocks, rows_ref, rhs_ref, inv_ref, upd_ref, fwd_ref, *rest):
    outs, (acc_a, acc_b, terms_a, terms_b) = rest[:2], rest[2:]
    step = pl.program_id(0)
    scenarios = rhs_ref.shape[0]
    count = upd_ref.shape[1]

    @pl.when(step == 0)
    def _():
        acc_a[...] = jnp.zeros_like(acc_a)
        acc_b[...] = jnp.zeros_like(acc_b)
        terms_b[...] = jnp.zeros_like(terms_b)

    def block(old, new):
        before = jnp.maximum(step - 1, 0)
        for index in range(count):
            acc = acc_a if index % 2 == 0 else acc_b
            row = rows_ref[before, index]
            acc[pl.ds(row, 1), :] += old[pl.ds(index, 1), :]
        forward = folded(product(stacked(rhs_ref[...]), inv_ref[0], 1), scenarios)
        fwd_ref[...] = forward
        left = stacked(forward)
        high, low = halves(upd_ref[0])
        dims = (((1,), (1,)), ((), ()))
        total = lax.dot_general(high, left, dims, preferred_element_type=F32)
        total = total + lax.dot_general(low, left, dims, preferred_element_type=F32)
        new[...] = total + pltpu.roll(total, PAD, 1)

    @pl.when(step % 2 == 0)
    def _():
        block(terms_b, terms_a)

    @pl.when(step % 2 == 1)
    def _():
        block(terms_a, terms_b)

    @pl.when(step == blocks)
    def _():
        width = outs[0].shape[-1]
        place = 0
        for out in outs:
            flat = [(g, b) for g in range(out.shape[0]) for b in range(out.shape[1])]
            for g, b in flat:
                piece = acc_a[pl.ds(place, width), :] + acc_b[pl.ds(place, width), :]
                out[g, b] = piece.T[:scenarios]
                place += width


def leaf_spread(rows, leaf_rhs, leaf_inverse, leaf_update, width):
    scenarios = leaf_rhs.shape[0]
    blocks, size, _ = leaf_inverse.shape
    count = leaf_update.shape[1]
    groups = [2, 4]
    total = sum(groups) * 4 * width
    shapes = [jax.ShapeDtypeStruct((4, g, scenarios, width), F32) for g in groups]
    return pl.pallas_call(
        functools.partial(spread_kernel, blocks),
        grid_spec=pltpu.PrefetchScalarGridSpec(
            num_scalar_prefetch=1,
            grid=(blocks + 1,),
            in_specs=[
                pl.BlockSpec((scenarios, size), lambda j, r: (0, jnp.minimum(j, blocks - 1))),
                pl.BlockSpec((1, size, size), lambda j, r: (jnp.minimum(j, blocks - 1), 0, 0)),
                pl.BlockSpec((1, count, size), lambda j, r: (jnp.minimum(j, blocks - 1), 0, 0)),
            ],
            out_specs=[pl.BlockSpec((scenarios, size), lambda j, r: (0, jnp.minimum(j, blocks - 1)))]
            + [pl.BlockSpec(x.shape, lambda j, r: (0, 0, 0, 0)) for x in shapes],
            scratch_shapes=[
                pltpu.VMEM((total, 128), F32),
                pltpu.VMEM((total, 128), F32),
                pltpu.VMEM((count, 128), F32),
                pltpu.VMEM((count, 128), F32),
            ],
        ),
        out_shape=[jax.ShapeDtypeStruct(leaf_rhs.shape, F32)] + shapes,
        compiler_params=pltpu.CompilerParams(vmem_limit_bytes=50 * 2**20),
    )(rows, leaf_rhs, leaf_inverse, leaf_update)


def finish_kernel(
    blocks, rows_ref, fwd_ref, inv_ref, upd_ref, mine, other, out_ref, table, found_a, found_b
):
    step = pl.program_id(0)
    scenarios = fwd_ref.shape[0]
    count = upd_ref.shape[1]

    @pl.when(step == 0)
    def _():
        width = mine.shape[-1]
        place = 0
        for source in (mine, other):
            for g in range(source.shape[0]):
                for b in range(source.shape[1]):
                    piece = jnp.concatenate(
                        [source[g, b], jnp.zeros((128 - scenarios, width), F32)], axis=0
                    )
                    table[pl.ds(place, width), :] = piece.T
                    place += width
        found_b[...] = jnp.zeros_like(found_b)

    def block(old, new):
        after = jnp.minimum(step, blocks - 1)
        for index in range(count):
            row = rows_ref[after, index]
            new[pl.ds(index, 1), :] = table[pl.ds(row, 1), :]
        targets = old[...].T[:scenarios]
        through = fwd_ref[...] - folded(product(stacked(targets), upd_ref[0], 0), scenarios)
        out_ref[...] = folded(product(stacked(through), inv_ref[0], 0), scenarios)

    @pl.when(step % 2 == 0)
    def _():
        block(found_b, found_a)

    @pl.when(step % 2 == 1)
    def _():
        block(found_a, found_b)


def leaf_finish(rows, forward, leaf_inverse, leaf_update, sources):
    scenarios = forward.shape[0]
    blocks, size, _ = leaf_inverse.shape
    count = leaf_update.shape[1]
    total = sum(x.shape[0] * x.shape[1] * x.shape[3] for x in sources)
    return pl.pallas_call(
        functools.partial(finish_kernel, blocks),
        grid_spec=pltpu.PrefetchScalarGridSpec(
            num_scalar_prefetch=1,
            grid=(blocks + 1,),
            in_specs=[
                pl.BlockSpec((scenarios, size), lambda j, r: (0, jnp.maximum(j - 1, 0))),
                pl.BlockSpec((1, size, size), lambda j, r: (jnp.maximum(j - 1, 0), 0, 0)),
                pl.BlockSpec((1, count, size), lambda j, r: (jnp.maximum(j - 1, 0), 0, 0)),
            ]
            + [pl.BlockSpec(x.shape, lambda j, r: (0, 0, 0, 0)) for x in sources],
            out_specs=pl.BlockSpec((scenarios, size), lambda j, r: (0, jnp.maximum(j - 1, 0))),
            scratch_shapes=[pltpu.VMEM((total, 128), F32)] + [pltpu.VMEM((count, 128), F32)] * 2,
        ),
        out_shape=jax.ShapeDtypeStruct(forward.shape, F32),
        compiler_params=pltpu.CompilerParams(vmem_limit_bytes=24 * 2**20),
    )(rows, forward, leaf_inverse, leaf_update, *sources)


def chain_kernel(mode, contract, long_dim, count, place_ref, *refs):
    x_refs, w_ref = refs[:count], refs[count]
    outs = refs[count + 1 : count + (5 if mode == "parts" else 2)]
    held, sems = refs[-2:]
    rows, width = x_refs[0].shape
    copies = []
    for j in range(4):
        if long_dim is None:
            source = w_ref.at[j]
        else:
            block = (place_ref[0] + (j if mode == "parts" else 4 - j)) % 4
            span = pl.ds(pl.multiple_of(block * width, width), width)
            source = w_ref.at[span, :] if long_dim == 0 else w_ref.at[:, span]
        copies.append(pltpu.make_async_copy(source, held.at[j], sems.at[j]))
        copies[-1].start()
    dims = (((1,), (contract,)), ((), ()))
    left = [stacked(x[...]) for x in x_refs]
    total = None
    for j in range(4):
        copies[j].wait()
        if long_dim is None:
            high, low = held[j, 0], held[j, 1]
        else:
            high, low = halves(held[j])
        mine = left[j % count]
        value = lax.dot_general(mine, high, dims, preferred_element_type=F32)
        value = value + lax.dot_general(mine, low, dims, preferred_element_type=F32)
        if mode == "parts":
            outs[j][...] = folded(value, rows)
        else:
            total = value if total is None else total + value
    if mode == "sum":
        outs[0][...] = folded(total, rows)


def chain_product(place, xs, weights, long_dim, contract, mode):
    rows, width = xs[0].shape
    number = 4 if mode == "parts" else 1
    held = (
        pltpu.VMEM((4, 2, width, width), BF16)
        if long_dim is None
        else pltpu.VMEM((4, width, width), F32)
    )
    whole = pl.BlockSpec(memory_space=pltpu.VMEM)
    result = pl.pallas_call(
        functools.partial(chain_kernel, mode, contract, long_dim, len(xs)),
        in_specs=[pl.BlockSpec(memory_space=pltpu.SMEM)]
        + [whole] * len(xs)
        + [pl.BlockSpec(memory_space=pltpu.HBM)],
        out_specs=[whole] * number,
        out_shape=[jax.ShapeDtypeStruct((rows, width), F32)] * number,
        scratch_shapes=[held, pltpu.SemaphoreType.DMA((4,))],
        compiler_params=pltpu.CompilerParams(vmem_limit_bytes=16 * 2**20),
        cost_estimate=pl.CostEstimate(
            flops=16 * rows * width * width, bytes_accessed=4 * 2**20, transcendentals=0
        ),
    )(place, *xs, weights)
    return result if mode == "parts" else result[0]


def squared_kernel(place_ref, *refs):
    x_refs, own_ref, after, far_upper, far_lower, before, out_ref, held, kept, sems = refs
    rows, width = out_ref.shape
    slots = held.shape[0]
    jobs = []
    for j, source in ((0, (own_ref,)), (1, (after,)), (3, (before,)), (2, (far_upper, far_lower))):
        each = 4 // len(source)
        for i in range(4):
            jobs.append((j, i, source[i // each].at[pl.ds(i % each * width, width), :]))
    copies = []
    for number, (j, i, block) in enumerate(jobs):
        target = kept.at[i] if number < 4 else held.at[number % slots]
        sem = sems.at[number % slots] if number >= 4 else sems.at[slots + number]
        copies.append(pltpu.make_async_copy(block, target, sem))
    for number in range(4 + slots):
        copies[number].start()
    left = [stacked(x[...]) for x in x_refs]
    totals = [None] * 4
    for number, (j, i, _) in enumerate(jobs):
        copies[number].wait()
        weights = kept[i] if number < 4 else held[number % slots]
        value = product(left[j], weights, 1)
        totals[i] = value if totals[i] is None else totals[i] + value
        if number >= 4 and number + slots < len(jobs):
            copies[number + slots].start()
    result = None
    for i in range(4):
        value = product(stacked(folded(totals[i], rows)), kept[i], 0)
        result = value if result is None else result + value
    out_ref[...] = folded(result, rows)


def squared_product(place, xs, own, others):
    rows, width = xs[0].shape
    slots = 4
    whole = pl.BlockSpec(memory_space=pltpu.VMEM)
    far = pl.BlockSpec(memory_space=pltpu.HBM)

    def body(place_ref, *refs):
        squared_kernel(place_ref, list(refs[:4]), *refs[4:])

    return pl.pallas_call(
        body,
        in_specs=[pl.BlockSpec(memory_space=pltpu.SMEM)] + [whole] * 4 + [far] * 5,
        out_specs=whole,
        out_shape=jax.ShapeDtypeStruct((rows, width), F32),
        scratch_shapes=[
            pltpu.VMEM((slots, width, width), F32),
            pltpu.VMEM((4, width, width), F32),
            pltpu.SemaphoreType.DMA((slots + 4,)),
        ],
        compiler_params=pltpu.CompilerParams(vmem_limit_bytes=60 * 2**20),
        cost_estimate=pl.CostEstimate(
            flops=80 * rows * width * width, bytes_accessed=16 * 2**20, transcendentals=0
        ),
    )(place, *xs, own, *others)


def half_copies(flag, after, before):
    rows, width = after.shape
    half = rows // 2

    def body(flag_ref, after_ref, before_ref, upper_ref, lower_ref, held, sems):
        @pl.when(flag_ref[0] == 1)
        def _():
            sources = after_ref.at[pl.ds(0, half), :], before_ref.at[pl.ds(half, half), :]
            inward = [pltpu.make_async_copy(sources[k], held.at[k], sems.at[k]) for k in (0, 1)]
            outward = [
                pltpu.make_async_copy(held.at[k], (upper_ref, lower_ref)[k], sems.at[2 + k])
                for k in (0, 1)
            ]
            for k in (0, 1):
                inward[k].start()
            for k in (0, 1):
                inward[k].wait()
                outward[k].start()
            for k in (0, 1):
                outward[k].wait()

    far = pl.BlockSpec(memory_space=pltpu.HBM)
    return pl.pallas_call(
        body,
        in_specs=[pl.BlockSpec(memory_space=pltpu.SMEM), far, far],
        out_specs=[far, far],
        out_shape=[jax.ShapeDtypeStruct((half, width), F32)] * 2,
        scratch_shapes=[pltpu.VMEM((2, half, width), F32), pltpu.SemaphoreType.DMA((4,))],
        compiler_params=pltpu.CompilerParams(vmem_limit_bytes=16 * 2**20),
    )(flag, after, before)


def merged(flag, a, groups, places, held):
    width = a.shape[0]
    pieces = [piece for group in groups for piece in group]
    extra = [] if held is None else [held]

    def body(flag_ref, a_ref, *refs):
        out_ref, left_held, right_held, result, sems = refs[len(pieces) + len(extra) :]
        sources, first = [], 0
        for group in groups:
            sources.append(refs[first : first + len(group)])
            first += len(group)

        @pl.when(flag_ref[0] == 1)
        def _():
            left_copies, right_copies = [], []
            for i in range(4):
                block = a_ref.at[:, pl.ds(i * width, width)]
                left_copies.append(pltpu.make_async_copy(block, left_held.at[i], sems.at[i]))
                left_copies[-1].start()
                block = place_block(sources[0], i)
                right_copies.append(
                    pltpu.make_async_copy(block, right_held.at[i], sems.at[4 + i])
                )
                right_copies[-1].start()
            for g in range(1, len(groups)):
                for i in range(4):
                    number = 4 * g + i
                    right_copies.append(
                        pltpu.make_async_copy(
                            place_block(sources[g], i), right_held.at[number], sems.at[4 + number]
                        )
                    )
                    right_copies[-1].start()
            dims = (((1,), (0,)), ((), ()))
            backs = []
            for g, place in enumerate(places):
                total = None
                for i in range(4):
                    if g == 0:
                        left_copies[i].wait()
                    right_copies[4 * g + i].wait()
                    left, right = halves(left_held[i]), halves(right_held[4 * g + i])
                    for x, y in ((0, 0), (0, 1), (1, 0)):
                        term = lax.dot_general(left[x], right[y], dims, preferred_element_type=F32)
                        total = term if total is None else total + term
                high, low = halves(total)
                result[g, 0] = high
                result[g, 1] = low
                backs.append(
                    pltpu.make_async_copy(
                        result.at[g], out_ref.at[place], sems.at[4 + 4 * len(groups) + g]
                    )
                )
                backs[-1].start()
            for back in backs:
                back.wait()

    def place_block(source, i):
        each = 4 // len(source)
        return source[i // each].at[pl.ds(i % each * width, width), :]

    far = pl.BlockSpec(memory_space=pltpu.HBM)
    return pl.pallas_call(
        body,
        in_specs=[pl.BlockSpec(memory_space=pltpu.SMEM)] + [far] * (1 + len(pieces) + len(extra)),
        out_specs=far,
        out_shape=jax.ShapeDtypeStruct((4, 2, width, width), BF16),
        scratch_shapes=[
            pltpu.VMEM((4, width, width), F32),
            pltpu.VMEM((4 * len(groups), width, width), F32),
            pltpu.VMEM((len(groups), 2, width, width), BF16),
            pltpu.SemaphoreType.DMA((4 + 5 * len(groups),)),
        ],
        input_output_aliases={} if held is None else {2 + len(pieces): 0},
        compiler_params=pltpu.CompilerParams(vmem_limit_bytes=28 * 2**20),
        cost_estimate=pl.CostEstimate(
            flops=24 * len(groups) * width**3, bytes_accessed=10 * 2**20, transcendentals=0
        ),
    )(flag, a, *pieces, *extra)


def joint_sent(value, pairs, core):
    count = lax.axis_size("leaf")
    full = [(a * 4 + x, a * 4 + y) for a in range(core, count, 2) for x, y in pairs]
    return lax.ppermute(value, JOINT, full)


def bulk_sent(value, steps, core):
    return joint_sent(value, [(x, (x + steps) % 4) for x in range(4)], core)


def swapped(value, mask, chosen=None):
    count = lax.axis_size("leaf")
    pairs = [(a, a ^ mask) for a in range(count) if chosen is None or chosen(a)]
    return lax.ppermute(value, "leaf", pairs)


def shifted(value, steps):
    count = lax.axis_size("sep")
    return lax.ppermute(value, "sep", [(a, (a + steps) % count) for a in range(count)])


def odd_shifted(value, steps):
    return joint_sent(value, [(x, (x + steps) % 4) for x in range(4)], 1)


def even_shifted(value, steps):
    return joint_sent(value, [(x, (x + steps) % 4) for x in range(4)], 0)


def sep_reduced(parts, sign=1, move=shifted):
    total = parts[0]
    for steps in (1, 2, 3):
        total = total + move(parts[steps], sign * steps % 4)
    return total


def sep_gathered(share, move=shifted):
    return [share, move(share, 1), move(share, 2), move(share, 3)]


def static_level(a):
    level = 1
    for bit in range(5):
        level += a % 2 ** (bit + 1) == 0
    return level


def level_of(index_now):
    total = jnp.ones_like(index_now)
    for bit in range(5):
        total = total + (index_now % 2 ** (bit + 1) == 0).astype(jnp.int32)
    return total


def on_device(leaf_rhs, leaf_inverse, leaf_update, leaf_rows, sep_rhs, sep_inverse, sep_update):
    scenarios, quarter = sep_rhs.shape
    width = sep_update.shape[1]
    home = lax.axis_index("leaf")
    member = lax.axis_index("sep")
    core = home % 2
    level = level_of(home)
    place = member.reshape(1).astype(jnp.int32)

    row_home, within = leaf_rows // width, leaf_rows % width
    part, rest = within // quarter, within % quarter
    at = level_of(row_home)
    turn = (part - member) % 4
    slot = jnp.where(at <= 2, turn * 2 + at - 1, turn * 4 + at + 5)
    add_at = slot * quarter + rest
    is_even = (at >= 2) & (at <= 4)
    slot = jnp.where(is_even, at - 2, jnp.where(at == 1, 0, at - 4))
    theirs = (is_even != (core == 0)).astype(jnp.int32)
    take_at = (theirs * 12 + (member - part) % 4 * 3 + slot) * quarter + rest

    leaf_forward, low, high = leaf_spread(
        add_at, leaf_rhs, leaf_inverse, leaf_update, quarter
    )
    low = low + swapped(low, 1)
    high = high + swapped(high, 1)
    even = lambda a: a % 2 == 0
    high = high + swapped(high, 2, even)

    flag = (core == 0).astype(jnp.int32).reshape(1)
    half = width // 2
    after = bulk_sent(sep_inverse, 1, 0)
    before = bulk_sent(sep_inverse, 3, 0)
    update = merged(flag, sep_update, [[sep_inverse]], [0], None)
    low, update, after, before = lax.optimization_barrier((low, update, after, before))

    low = sep_reduced([low[j] for j in range(4)], move=odd_shifted)
    one = chain_product(place, [sep_rhs - low[0]], sep_inverse, 0, 1, "parts")
    halves_out = half_copies(flag, after, before)
    halves_out, update = lax.optimization_barrier((halves_out, update))
    far_upper = bulk_sent(halves_out[0], 1, 0)
    far_lower = bulk_sent(halves_out[1], 3, 0)
    update = merged(flag, sep_update, [[after], [before]], [1, 3], update)
    high = high + swapped(high, 4, even)
    high, update = lax.optimization_barrier((high, update))
    high = [high[0]] + [even_shifted(high[j], j) for j in (1, 2, 3)]
    update = merged(flag, sep_update, [[far_upper, far_lower]], [2], update)
    high, update = lax.optimization_barrier((high, update))
    high = high[0] + high[1] + high[2] + high[3]

    forward_one = sep_reduced(one, move=odd_shifted)
    moved = chain_product(place, sep_gathered(forward_one, odd_shifted), sep_update, 1, 1, "sum")
    moved = moved + low[1]
    moved, update, high = lax.optimization_barrier((moved, update, high))
    moved = swapped(moved + swapped(moved, 2), 1)

    def to_parent(moved, section):
        reach = 2 ** (section - 1)
        if section == 5:
            return swapped(moved, 16)
        return swapped(moved, reach) + swapped(moved, 3 * reach)

    def from_parent(value, section, chosen=None):
        reach = 2 ** (section - 1)
        if section == 5:
            return swapped(value, 16, chosen)
        left_side = home // (2 * reach) % 2 == 0
        return jnp.where(
            left_side, swapped(value, 3 * reach, chosen), swapped(value, reach, chosen)
        )

    pending = sep_rhs - jnp.where(level == 2, moved, 0.0)
    for section in range(2, 6):
        moved = chain_product(place, sep_gathered(pending), update, None, 1, "sum")
        moved, high = lax.optimization_barrier((moved, high))
        if section == 2:
            spread = {3: high[0]}
            high = high[1:] + swapped(high[1:], 8, even)
        elif section == 3:
            spread[4] = high[0]
            high = high[1:] + swapped(high[1:], 16, even)
            spread[5], spread[6] = high[0], high[1]
        arriving = to_parent(moved, section) + spread[section + 1]
        pending = pending - jnp.where(level == section + 1, arriving, 0.0)
    squared = squared_product(
        place, sep_gathered(pending), sep_inverse, [after, far_upper, far_lower, before]
    )

    own_solution = squared
    above = None
    for section in range(5, 0, -1):
        parent = from_parent(own_solution, section)
        if section == 1:
            above = from_parent(above, section, chosen=lambda a: static_level(a) == 2)
            above = jnp.concatenate([parent[None], above])
            above = jnp.where(core == 0, swapped(above, 1), above)
        elif above is None:
            above = parent[None]
        else:
            chosen = lambda a: static_level(a) == section + 1
            above = jnp.concatenate([parent[None], from_parent(above, section, chosen)])
        if section > 1:
            result = squared - sep_reduced(
                chain_product(place, [parent], update, None, 0, "parts"), -1
            )
        else:
            through = forward_one - sep_reduced(
                chain_product(place, [parent], sep_update, 1, 0, "parts")
            )
            result = chain_product(place, sep_gathered(through), sep_inverse, 0, 0, "sum")
        own_solution = jnp.where(level == section, result, own_solution)

    own_three = jnp.concatenate([own_solution[None], above[3:5]])
    mine = jnp.stack(sep_gathered(jnp.where(core == 0, above[0:3], own_three)))
    leaf_solution = leaf_finish(
        take_at,
        leaf_forward,
        leaf_inverse,
        leaf_update,
        [mine, swapped(mine, 1)],
    )
    return leaf_solution, own_solution


def solution(mesh):
    return jax.shard_map(
        on_device,
        mesh=mesh,
        in_specs=(
            P(None, JOINT),
            P(JOINT, None, None),
            P(JOINT, None, None),
            P(JOINT, None),
            P(None, JOINT),
            P(None, JOINT),
            P(JOINT, None),
        ),
        out_specs=(P(None, JOINT), P(None, JOINT)),
        check_vma=False,
    )
```

```python
import functools

import jax
import jax.numpy as jnp
from jax import lax
from jax.experimental import pallas as pl
from jax.experimental.pallas import tpu as pltpu
from jax.sharding import PartitionSpec as P

JOINT = ("leaf", "sep")
PAD = 64
F32 = jnp.float32
BF16 = jnp.bfloat16


def halves(value):
    high = value.astype(BF16)
    low = (value - high.astype(F32)).astype(BF16)
    return high, low


def stacked(value):
    rows, width = value.shape
    padded = jnp.concatenate([value, jnp.zeros((PAD - rows, width), F32)], axis=0)
    high, low = halves(padded)
    return jnp.concatenate([high, low], axis=0)


def product(left, weights, contract):
    high, low = halves(weights)
    dims = (((1,), (contract,)), ((), ()))
    total = lax.dot_general(left, high, dims, preferred_element_type=F32)
    return total + lax.dot_general(left, low, dims, preferred_element_type=F32)


def folded(total, rows):
    return total[:rows] + total[PAD : PAD + rows]


def spread_kernel(blocks, rows_ref, rhs_ref, inv_ref, upd_ref, fwd_ref, *rest):
    outs, (acc_a, acc_b, terms_a, terms_b) = rest[:2], rest[2:]
    step = pl.program_id(0)
    scenarios = rhs_ref.shape[0]
    count = upd_ref.shape[1]

    @pl.when(step == 0)
    def _():
        acc_a[...] = jnp.zeros_like(acc_a)
        acc_b[...] = jnp.zeros_like(acc_b)
        terms_b[...] = jnp.zeros_like(terms_b)

    def block(old, new):
        before = jnp.maximum(step - 1, 0)
        for index in range(count):
            acc = acc_a if index % 2 == 0 else acc_b
            row = rows_ref[before, index]
            acc[pl.ds(row, 1), :] += old[pl.ds(index, 1), :]
        forward = folded(product(stacked(rhs_ref[...]), inv_ref[0], 1), scenarios)
        fwd_ref[...] = forward
        left = stacked(forward)
        high, low = halves(upd_ref[0])
        dims = (((1,), (1,)), ((), ()))
        total = lax.dot_general(high, left, dims, preferred_element_type=F32)
        total = total + lax.dot_general(low, left, dims, preferred_element_type=F32)
        new[...] = total + pltpu.roll(total, PAD, 1)

    @pl.when(step % 2 == 0)
    def _():
        block(terms_b, terms_a)

    @pl.when(step % 2 == 1)
    def _():
        block(terms_a, terms_b)

    @pl.when(step == blocks)
    def _():
        width = outs[0].shape[-1]
        place = 0
        for out in outs:
            flat = [(g, b) for g in range(out.shape[0]) for b in range(out.shape[1])]
            for g, b in flat:
                piece = acc_a[pl.ds(place, width), :] + acc_b[pl.ds(place, width), :]
                out[g, b] = piece.T[:scenarios]
                place += width


def leaf_spread(rows, leaf_rhs, leaf_inverse, leaf_update, width):
    scenarios = leaf_rhs.shape[0]
    blocks, size, _ = leaf_inverse.shape
    count = leaf_update.shape[1]
    groups = [2, 4]
    total = sum(groups) * 4 * width
    shapes = [jax.ShapeDtypeStruct((4, g, scenarios, width), F32) for g in groups]
    return pl.pallas_call(
        functools.partial(spread_kernel, blocks),
        grid_spec=pltpu.PrefetchScalarGridSpec(
            num_scalar_prefetch=1,
            grid=(blocks + 1,),
            in_specs=[
                pl.BlockSpec((scenarios, size), lambda j, r: (0, jnp.minimum(j, blocks - 1))),
                pl.BlockSpec((1, size, size), lambda j, r: (jnp.minimum(j, blocks - 1), 0, 0)),
                pl.BlockSpec((1, count, size), lambda j, r: (jnp.minimum(j, blocks - 1), 0, 0)),
            ],
            out_specs=[pl.BlockSpec((scenarios, size), lambda j, r: (0, jnp.minimum(j, blocks - 1)))]
            + [pl.BlockSpec(x.shape, lambda j, r: (0, 0, 0, 0)) for x in shapes],
            scratch_shapes=[
                pltpu.VMEM((total, 128), F32),
                pltpu.VMEM((total, 128), F32),
                pltpu.VMEM((count, 128), F32),
                pltpu.VMEM((count, 128), F32),
            ],
        ),
        out_shape=[jax.ShapeDtypeStruct(leaf_rhs.shape, F32)] + shapes,
        compiler_params=pltpu.CompilerParams(vmem_limit_bytes=50 * 2**20),
    )(rows, leaf_rhs, leaf_inverse, leaf_update)


def finish_kernel(
    blocks, rows_ref, fwd_ref, inv_ref, upd_ref, mine, other, out_ref, table, found_a, found_b
):
    step = pl.program_id(0)
    scenarios = fwd_ref.shape[0]
    count = upd_ref.shape[1]

    @pl.when(step == 0)
    def _():
        width = mine.shape[-1]
        place = 0
        for source in (mine, other):
            for g in range(source.shape[0]):
                for b in range(source.shape[1]):
                    piece = jnp.concatenate(
                        [source[g, b], jnp.zeros((128 - scenarios, width), F32)], axis=0
                    )
                    table[pl.ds(place, width), :] = piece.T
                    place += width
        found_b[...] = jnp.zeros_like(found_b)

    def block(old, new):
        after = jnp.minimum(step, blocks - 1)
        for index in range(count):
            row = rows_ref[after, index]
            new[pl.ds(index, 1), :] = table[pl.ds(row, 1), :]
        targets = old[...].T[:scenarios]
        through = fwd_ref[...] - folded(product(stacked(targets), upd_ref[0], 0), scenarios)
        out_ref[...] = folded(product(stacked(through), inv_ref[0], 0), scenarios)

    @pl.when(step % 2 == 0)
    def _():
        block(found_b, found_a)

    @pl.when(step % 2 == 1)
    def _():
        block(found_a, found_b)


def leaf_finish(rows, forward, leaf_inverse, leaf_update, sources):
    scenarios = forward.shape[0]
    blocks, size, _ = leaf_inverse.shape
    count = leaf_update.shape[1]
    total = sum(x.shape[0] * x.shape[1] * x.shape[3] for x in sources)
    return pl.pallas_call(
        functools.partial(finish_kernel, blocks),
        grid_spec=pltpu.PrefetchScalarGridSpec(
            num_scalar_prefetch=1,
            grid=(blocks + 1,),
            in_specs=[
                pl.BlockSpec((scenarios, size), lambda j, r: (0, jnp.maximum(j - 1, 0))),
                pl.BlockSpec((1, size, size), lambda j, r: (jnp.maximum(j - 1, 0), 0, 0)),
                pl.BlockSpec((1, count, size), lambda j, r: (jnp.maximum(j - 1, 0), 0, 0)),
            ]
            + [pl.BlockSpec(x.shape, lambda j, r: (0, 0, 0, 0)) for x in sources],
            out_specs=pl.BlockSpec((scenarios, size), lambda j, r: (0, jnp.maximum(j - 1, 0))),
            scratch_shapes=[pltpu.VMEM((total, 128), F32)] + [pltpu.VMEM((count, 128), F32)] * 2,
        ),
        out_shape=jax.ShapeDtypeStruct(forward.shape, F32),
        compiler_params=pltpu.CompilerParams(vmem_limit_bytes=24 * 2**20),
    )(rows, forward, leaf_inverse, leaf_update, *sources)


def chain_kernel(mode, contract, long_dim, count, place_ref, *refs):
    x_refs, w_ref = refs[:count], refs[count]
    outs = refs[count + 1 : count + (5 if mode == "parts" else 2)]
    held, sems = refs[-2:]
    rows, width = x_refs[0].shape
    copies = []
    for j in range(4):
        if long_dim is None:
            source = w_ref.at[j]
        else:
            block = (place_ref[0] + (j if mode == "parts" else 4 - j)) % 4
            span = pl.ds(pl.multiple_of(block * width, width), width)
            source = w_ref.at[span, :] if long_dim == 0 else w_ref.at[:, span]
        copies.append(pltpu.make_async_copy(source, held.at[j], sems.at[j]))
        copies[-1].start()
    dims = (((1,), (contract,)), ((), ()))
    left = [stacked(x[...]) for x in x_refs]
    total = None
    for j in range(4):
        copies[j].wait()
        if long_dim is None:
            high, low = held[j, 0], held[j, 1]
        else:
            high, low = halves(held[j])
        mine = left[j % count]
        value = lax.dot_general(mine, high, dims, preferred_element_type=F32)
        value = value + lax.dot_general(mine, low, dims, preferred_element_type=F32)
        if mode == "parts":
            outs[j][...] = folded(value, rows)
        else:
            total = value if total is None else total + value
    if mode == "sum":
        outs[0][...] = folded(total, rows)


def chain_product(place, xs, weights, long_dim, contract, mode):
    rows, width = xs[0].shape
    number = 4 if mode == "parts" else 1
    held = (
        pltpu.VMEM((4, 2, width, width), BF16)
        if long_dim is None
        else pltpu.VMEM((4, width, width), F32)
    )
    whole = pl.BlockSpec(memory_space=pltpu.VMEM)
    result = pl.pallas_call(
        functools.partial(chain_kernel, mode, contract, long_dim, len(xs)),
        in_specs=[pl.BlockSpec(memory_space=pltpu.SMEM)]
        + [whole] * len(xs)
        + [pl.BlockSpec(memory_space=pltpu.HBM)],
        out_specs=[whole] * number,
        out_shape=[jax.ShapeDtypeStruct((rows, width), F32)] * number,
        scratch_shapes=[held, pltpu.SemaphoreType.DMA((4,))],
        compiler_params=pltpu.CompilerParams(vmem_limit_bytes=16 * 2**20),
        cost_estimate=pl.CostEstimate(
            flops=16 * rows * width * width, bytes_accessed=4 * 2**20, transcendentals=0
        ),
    )(place, *xs, weights)
    return result if mode == "parts" else result[0]


def squared_kernel(place_ref, *refs):
    x_refs, own_ref, after, far_upper, far_lower, before, out_ref, held, kept, sems = refs
    rows, width = out_ref.shape
    slots = held.shape[0]
    jobs = []
    for j, source in ((0, (own_ref,)), (1, (after,)), (3, (before,)), (2, (far_upper, far_lower))):
        each = 4 // len(source)
        for i in range(4):
            jobs.append((j, i, source[i // each].at[pl.ds(i % each * width, width), :]))
    copies = []
    for number, (j, i, block) in enumerate(jobs):
        target = kept.at[i] if number < 4 else held.at[number % slots]
        sem = sems.at[number % slots] if number >= 4 else sems.at[slots + number]
        copies.append(pltpu.make_async_copy(block, target, sem))
    for number in range(4 + slots):
        copies[number].start()
    left = [stacked(x[...]) for x in x_refs]
    totals = [None] * 4
    for number, (j, i, _) in enumerate(jobs):
        copies[number].wait()
        weights = kept[i] if number < 4 else held[number % slots]
        value = product(left[j], weights, 1)
        totals[i] = value if totals[i] is None else totals[i] + value
        if number >= 4 and number + slots < len(jobs):
            copies[number + slots].start()
    result = None
    for i in range(4):
        value = product(stacked(folded(totals[i], rows)), kept[i], 0)
        result = value if result is None else result + value
    out_ref[...] = folded(result, rows)


def squared_product(place, xs, own, others):
    rows, width = xs[0].shape
    slots = 4
    whole = pl.BlockSpec(memory_space=pltpu.VMEM)
    far = pl.BlockSpec(memory_space=pltpu.HBM)

    def body(place_ref, *refs):
        squared_kernel(place_ref, list(refs[:4]), *refs[4:])

    return pl.pallas_call(
        body,
        in_specs=[pl.BlockSpec(memory_space=pltpu.SMEM)] + [whole] * 4 + [far] * 5,
        out_specs=whole,
        out_shape=jax.ShapeDtypeStruct((rows, width), F32),
        scratch_shapes=[
            pltpu.VMEM((slots, width, width), F32),
            pltpu.VMEM((4, width, width), F32),
            pltpu.SemaphoreType.DMA((slots + 4,)),
        ],
        compiler_params=pltpu.CompilerParams(vmem_limit_bytes=60 * 2**20),
        cost_estimate=pl.CostEstimate(
            flops=80 * rows * width * width, bytes_accessed=16 * 2**20, transcendentals=0
        ),
    )(place, *xs, own, *others)


def half_copies(flag, after, before):
    rows, width = after.shape
    half = rows // 2

    def body(flag_ref, after_ref, before_ref, upper_ref, lower_ref, held, sems):
        @pl.when(flag_ref[0] == 1)
        def _():
            sources = after_ref.at[pl.ds(0, half), :], before_ref.at[pl.ds(half, half), :]
            inward = [pltpu.make_async_copy(sources[k], held.at[k], sems.at[k]) for k in (0, 1)]
            outward = [
                pltpu.make_async_copy(held.at[k], (upper_ref, lower_ref)[k], sems.at[2 + k])
                for k in (0, 1)
            ]
            for k in (0, 1):
                inward[k].start()
            for k in (0, 1):
                inward[k].wait()
                outward[k].start()
            for k in (0, 1):
                outward[k].wait()

    far = pl.BlockSpec(memory_space=pltpu.HBM)
    return pl.pallas_call(
        body,
        in_specs=[pl.BlockSpec(memory_space=pltpu.SMEM), far, far],
        out_specs=[far, far],
        out_shape=[jax.ShapeDtypeStruct((half, width), F32)] * 2,
        scratch_shapes=[pltpu.VMEM((2, half, width), F32), pltpu.SemaphoreType.DMA((4,))],
        compiler_params=pltpu.CompilerParams(vmem_limit_bytes=16 * 2**20),
    )(flag, after, before)


def merged(flag, a, groups, places, held):
    width = a.shape[0]
    pieces = [piece for group in groups for piece in group]
    extra = [] if held is None else [held]

    def body(flag_ref, a_ref, *refs):
        out_ref, left_held, right_held, result, sems = refs[len(pieces) + len(extra) :]
        sources, first = [], 0
        for group in groups:
            sources.append(refs[first : first + len(group)])
            first += len(group)

        @pl.when(flag_ref[0] == 1)
        def _():
            left_copies, right_copies = [], []
            for i in range(4):
                block = a_ref.at[:, pl.ds(i * width, width)]
                left_copies.append(pltpu.make_async_copy(block, left_held.at[i], sems.at[i]))
                left_copies[-1].start()
                block = place_block(sources[0], i)
                right_copies.append(
                    pltpu.make_async_copy(block, right_held.at[i], sems.at[4 + i])
                )
                right_copies[-1].start()
            for g in range(1, len(groups)):
                for i in range(4):
                    number = 4 * g + i
                    right_copies.append(
                        pltpu.make_async_copy(
                            place_block(sources[g], i), right_held.at[number], sems.at[4 + number]
                        )
                    )
                    right_copies[-1].start()
            dims = (((1,), (0,)), ((), ()))
            backs = []
            for g, place in enumerate(places):
                total = None
                for i in range(4):
                    if g == 0:
                        left_copies[i].wait()
                    right_copies[4 * g + i].wait()
                    left, right = halves(left_held[i]), halves(right_held[4 * g + i])
                    for x, y in ((0, 0), (0, 1), (1, 0)):
                        term = lax.dot_general(left[x], right[y], dims, preferred_element_type=F32)
                        total = term if total is None else total + term
                high, low = halves(total)
                result[g, 0] = high
                result[g, 1] = low
                backs.append(
                    pltpu.make_async_copy(
                        result.at[g], out_ref.at[place], sems.at[4 + 4 * len(groups) + g]
                    )
                )
                backs[-1].start()
            for back in backs:
                back.wait()

    def place_block(source, i):
        each = 4 // len(source)
        return source[i // each].at[pl.ds(i % each * width, width), :]

    far = pl.BlockSpec(memory_space=pltpu.HBM)
    return pl.pallas_call(
        body,
        in_specs=[pl.BlockSpec(memory_space=pltpu.SMEM)] + [far] * (1 + len(pieces) + len(extra)),
        out_specs=far,
        out_shape=jax.ShapeDtypeStruct((4, 2, width, width), BF16),
        scratch_shapes=[
            pltpu.VMEM((4, width, width), F32),
            pltpu.VMEM((4 * len(groups), width, width), F32),
            pltpu.VMEM((len(groups), 2, width, width), BF16),
            pltpu.SemaphoreType.DMA((4 + 5 * len(groups),)),
        ],
        input_output_aliases={} if held is None else {2 + len(pieces): 0},
        compiler_params=pltpu.CompilerParams(vmem_limit_bytes=28 * 2**20),
        cost_estimate=pl.CostEstimate(
            flops=24 * len(groups) * width**3, bytes_accessed=10 * 2**20, transcendentals=0
        ),
    )(flag, a, *pieces, *extra)


def joint_sent(value, pairs, core):
    count = lax.axis_size("leaf")
    full = [(a * 4 + x, a * 4 + y) for a in range(core, count, 2) for x, y in pairs]
    return lax.ppermute(value, JOINT, full)


def bulk_sent(value, steps, core):
    return joint_sent(value, [(x, (x + steps) % 4) for x in range(4)], core)


def swapped(value, mask, chosen=None):
    count = lax.axis_size("leaf")
    pairs = [(a, a ^ mask) for a in range(count) if chosen is None or chosen(a)]
    return lax.ppermute(value, "leaf", pairs)


def shifted(value, steps):
    count = lax.axis_size("sep")
    return lax.ppermute(value, "sep", [(a, (a + steps) % count) for a in range(count)])


def odd_shifted(value, steps):
    return joint_sent(value, [(x, (x + steps) % 4) for x in range(4)], 1)


def even_shifted(value, steps):
    return joint_sent(value, [(x, (x + steps) % 4) for x in range(4)], 0)


def sep_reduced(parts, sign=1, move=shifted):
    total = parts[0]
    for steps in (1, 2, 3):
        total = total + move(parts[steps], sign * steps % 4)
    return total


def sep_gathered(share, move=shifted):
    return [share, move(share, 1), move(share, 2), move(share, 3)]


def static_level(a):
    level = 1
    for bit in range(5):
        level += a % 2 ** (bit + 1) == 0
    return level


def level_of(index_now):
    total = jnp.ones_like(index_now)
    for bit in range(5):
        total = total + (index_now % 2 ** (bit + 1) == 0).astype(jnp.int32)
    return total


def on_device(leaf_rhs, leaf_inverse, leaf_update, leaf_rows, sep_rhs, sep_inverse, sep_update):
    scenarios, quarter = sep_rhs.shape
    width = sep_update.shape[1]
    home = lax.axis_index("leaf")
    member = lax.axis_index("sep")
    core = home % 2
    level = level_of(home)
    place = member.reshape(1).astype(jnp.int32)

    row_home, within = leaf_rows // width, leaf_rows % width
    part, rest = within // quarter, within % quarter
    at = level_of(row_home)
    turn = (part - member) % 4
    slot = jnp.where(at <= 2, turn * 2 + at - 1, turn * 4 + at + 5)
    add_at = slot * quarter + rest
    is_even = (at >= 2) & (at <= 4)
    slot = jnp.where(is_even, at - 2, jnp.where(at == 1, 0, at - 4))
    theirs = (is_even != (core == 0)).astype(jnp.int32)
    take_at = (theirs * 12 + (member - part) % 4 * 3 + slot) * quarter + rest

    leaf_forward, low, high = leaf_spread(
        add_at, leaf_rhs, leaf_inverse, leaf_update, quarter
    )
    low = low + swapped(low, 1)
    high = high + swapped(high, 1)
    even = lambda a: a % 2 == 0
    high = high + swapped(high, 2, even)

    flag = (core == 0).astype(jnp.int32).reshape(1)
    half = width // 2
    after = bulk_sent(sep_inverse, 1, 0)
    before = bulk_sent(sep_inverse, 3, 0)
    update = merged(flag, sep_update, [[sep_inverse]], [0], None)
    low, update, after, before = lax.optimization_barrier((low, update, after, before))

    low = sep_reduced([low[j] for j in range(4)], move=odd_shifted)
    one = chain_product(place, [sep_rhs - low[0]], sep_inverse, 0, 1, "parts")
    halves_out = half_copies(flag, after, before)
    halves_out, update = lax.optimization_barrier((halves_out, update))
    far_upper = bulk_sent(halves_out[0], 1, 0)
    far_lower = bulk_sent(halves_out[1], 3, 0)
    update = merged(flag, sep_update, [[after], [before]], [1, 3], update)
    high = high + swapped(high, 4, even)
    high, update = lax.optimization_barrier((high, update))
    update = merged(flag, sep_update, [[far_upper, far_lower]], [2], update)

    forward_one = sep_reduced(one, move=odd_shifted)
    moved = chain_product(place, sep_gathered(forward_one, odd_shifted), sep_update, 1, 1, "sum")
    moved = moved + low[1]
    moved, update = lax.optimization_barrier((moved, update))
    moved = swapped(moved + swapped(moved, 2), 1)

    def to_parent(moved, section):
        reach = 2 ** (section - 1)
        if section == 5:
            return swapped(moved, 16)
        return swapped(moved, reach) + swapped(moved, 3 * reach)

    def from_parent(value, section, chosen=None):
        reach = 2 ** (section - 1)
        if section == 5:
            return swapped(value, 16, chosen)
        left_side = home // (2 * reach) % 2 == 0
        return jnp.where(
            left_side, swapped(value, 3 * reach, chosen), swapped(value, reach, chosen)
        )

    pending = sep_rhs - jnp.where(level == 2, moved, 0.0)
    for section in range(2, 6):
        gathered = sep_gathered(pending)
        if section == 2:
            gathered, high = lax.optimization_barrier((gathered, high))
            high = sep_reduced([high[j] for j in range(4)], move=even_shifted)
        moved = chain_product(place, gathered, update, None, 1, "sum")
        if section > 2:
            moved, high = lax.optimization_barrier((moved, high))
        if section == 2:
            spread = {3: high[0]}
            high = high[1:] + swapped(high[1:], 8, even)
        elif section == 3:
            spread[4] = high[0]
            high = high[1:] + swapped(high[1:], 16, even)
            spread[5], spread[6] = high[0], high[1]
        arriving = to_parent(moved, section) + spread[section + 1]
        pending = pending - jnp.where(level == section + 1, arriving, 0.0)
    squared = squared_product(
        place, sep_gathered(pending), sep_inverse, [after, far_upper, far_lower, before]
    )

    own_solution = squared
    above = None
    for section in range(5, 0, -1):
        parent = from_parent(own_solution, section)
        if section == 1:
            above = from_parent(above, section, chosen=lambda a: static_level(a) == 2)
            above = jnp.concatenate([parent[None], above])
            above = jnp.where(core == 0, swapped(above, 1), above)
        elif above is None:
            above = parent[None]
        else:
            chosen = lambda a: static_level(a) == section + 1
            above = jnp.concatenate([parent[None], from_parent(above, section, chosen)])
        if section > 1:
            result = squared - sep_reduced(
                chain_product(place, [parent], update, None, 0, "parts"), -1
            )
        else:
            through = forward_one - sep_reduced(
                chain_product(place, [parent], sep_update, 1, 0, "parts")
            )
            result = chain_product(place, sep_gathered(through), sep_inverse, 0, 0, "sum")
        own_solution = jnp.where(level == section, result, own_solution)

    own_three = jnp.concatenate([own_solution[None], above[3:5]])
    mine = jnp.stack(sep_gathered(jnp.where(core == 0, above[0:3], own_three)))
    leaf_solution = leaf_finish(
        take_at,
        leaf_forward,
        leaf_inverse,
        leaf_update,
        [mine, swapped(mine, 1)],
    )
    return leaf_solution, own_solution


def solution(mesh):
    return jax.shard_map(
        on_device,
        mesh=mesh,
        in_specs=(
            P(None, JOINT),
            P(JOINT, None, None),
            P(JOINT, None, None),
            P(JOINT, None),
            P(None, JOINT),
            P(None, JOINT),
            P(JOINT, None),
        ),
        out_specs=(P(None, JOINT), P(None, JOINT)),
        check_vma=False,
    )
```
